32 devices in a mesh: freq: 4 (over y, core), trace: 8 (over z, x).
Axes of the slice: x: 2, y: 2, z: 4, core: 2. Of those that a mesh axis runs over, the one named last changes fastest.
Arguments:
- traces: bfloat16 [4, 2048, 4096], P('freq', 'trace'), may hold values from -6 to 6
- coords: int32 [4, 4, 2048], replicated, may hold values from 0 to 1023
- wavenumbers: int32 [4, 4, 4096], replicated, may hold values from 0 to 1023
- fold: int32 [4], replicated, may hold values from 256 to 2048, as said below
- selected: int32 [2, 4, 1024], P(None, None, 'freq'), may hold values from 0 to 4095
Outputs:
- spectrum: float32 [4096, 4, 2, 1024], P('trace', None, None, 'freq')
- coefficients: float32 [2, 4, 2, 1024], P(None, None, None, 'freq')
The draws below stay inside these ranges and needn't reach their ends.
Inputs may be any that keep to these rules, and one draw needn't show every extreme that they name: Slots 0 to fold - 1 of a patch are live, the rest are not; some patch has all 2048 slots live.
All inputs are finite; a program needn't handle non-finite values.
Results may differ from the reference program's by a relative error of at most 0.0052.
Values may be sent and summed in bfloat16 or wider, within the bound.
A program may use at most 128 MiB of HBM per device.

```python
import math
import jax
import jax.numpy as jnp
from jax import lax

NT = 4096
NF = 1024
NK = 4096
GRID = 1024
ITERS = 2
PATCHES = 4
FOLD = 2048


def draw_fold(key, part):
    first = jax.random.fold_in(key, 11)
    second = jax.random.fold_in(key, 23)
    base = jax.random.randint(first, (PATCHES,), FOLD // 8, FOLD + 1)
    fullest = jax.random.randint(second, (), 0, PATCHES)
    return jnp.where(jnp.arange(PATCHES, dtype=jnp.int32) == fullest, FOLD, base).astype(jnp.int32)


def plant(drawn, rng, low, top_value):
    shape = drawn.shape
    spot = [jax.random.randint(jax.random.fold_in(rng, axis), (), 0, shape[axis]) for axis in range(len(shape))]
    drawn = drawn.at[tuple(spot)].set(low)
    longest = shape.index(max(shape))
    spot[longest] = (spot[longest] + 1) % shape[longest]
    return drawn.at[tuple(spot)].set(top_value)


def block_levels(key, extent, pieces, smallest, top_value):
    loudness, own = 1.0, jax.random.fold_in(key, 6)
    for dim, blocks in pieces:
        steps = jnp.exp(jax.random.uniform(jax.random.fold_in(own, dim), (blocks,), jnp.float32, smallest / len(pieces), top_value / len(pieces)))
        loudness = loudness * jnp.repeat(steps, extent[dim] // blocks).reshape([-1 if axis == dim else 1 for axis in range(len(extent))])
    return loudness


def scatter_about(key, shape, scale, bound, pieces=(), held_as=jnp.bfloat16):
    factor_of = block_levels(key, shape, pieces, -0.22, 0.18) if pieces else 1.0
    entries = jax.random.normal(key, shape, jnp.float32) * scale * factor_of
    return jnp.minimum(jnp.maximum(entries, -bound), bound).astype(held_as)


def setup_inputs(seed: int = 0) -> dict:
    seeds = jax.random.split(jax.random.key(seed), 6)
    return {
        "traces": scatter_about(seeds[0], (PATCHES, FOLD, NT), 1.0, 6.0, ((0, 4), (1, 8))),
        "coords": plant(jax.random.randint(seeds[1], (4, PATCHES, FOLD), 0, GRID), jax.random.fold_in(seeds[1], 1), 0, GRID - 1).astype(jnp.int32),
        "wavenumbers": plant(jax.random.randint(seeds[2], (4, PATCHES, NK), 0, GRID), jax.random.fold_in(seeds[2], 1), 0, GRID - 1).astype(jnp.int32),
        "fold": draw_fold(jax.random.fold_in(seeds[5], 71), 0),
        "selected": plant(jax.random.randint(seeds[4], (ITERS, PATCHES, NF), 0, NK), jax.random.fold_in(seeds[4], 1), 0, NK - 1).astype(jnp.int32),
    }


def dft_table(length, count):
    sample = jnp.arange(length, dtype=jnp.int32)
    bins = jnp.arange(count, dtype=jnp.int32)
    product = (sample[:, None] * bins[None, :]) % length
    angle = product.astype(jnp.float32) * (2.0 * math.pi / length)
    return jnp.concatenate([jnp.cos(angle), -jnp.sin(angle)], axis=1).astype(jnp.bfloat16)


def one_patch(inputs):
    rows, places, waves = inputs
    inner = jnp.zeros((waves.shape[1], places.shape[1]), jnp.int32)
    for comp in range(4):
        inner = inner + waves[comp][:, None] * places[comp][None, :]
    inner = inner % GRID
    angle = inner.astype(jnp.float32) * (2.0 * math.pi / GRID)
    atoms = jnp.concatenate([jnp.cos(angle), jnp.sin(angle)], axis=0).astype(jnp.bfloat16)
    product = jnp.dot(atoms, rows, preferred_element_type=jnp.float32)
    cand = waves.shape[1]
    s_real = product[:cand, :NF] + product[cand:, NF:]
    s_imag = product[:cand, NF:] - product[cand:, :NF]
    return jnp.stack([s_real, s_imag], axis=1)


def reference(traces, coords, wavenumbers, fold, selected):
    patches, slots, length = traces.shape
    table = dft_table(length, NF)
    spectra = jnp.dot(traces.reshape(patches * slots, length), table, preferred_element_type=jnp.float32)
    spectra = spectra.astype(jnp.bfloat16).reshape(patches, slots, 2, NF)
    live = (jnp.arange(slots, dtype=jnp.int32)[None, :] < fold[:, None]).astype(jnp.float32)
    res_real = spectra[:, :, 0, :].astype(jnp.float32) * live[:, :, None]
    res_imag = spectra[:, :, 1, :].astype(jnp.float32) * live[:, :, None]
    inverse = 1.0 / fold.astype(jnp.float32)
    gathered = []
    for iteration in range(ITERS):
        chosen = selected[iteration].astype(jnp.int32)
        picked = jnp.take_along_axis(wavenumbers, jnp.broadcast_to(chosen[None], (4,) + chosen.shape), axis=2)
        inner = jnp.zeros((patches, slots, NF), jnp.int32)
        for comp in range(4):
            inner = inner + picked[comp][:, None, :] * coords[comp][:, :, None]
        inner = inner % GRID
        angle = inner.astype(jnp.float32) * (2.0 * math.pi / GRID)
        cosine = jnp.cos(angle)
        sine = jnp.sin(angle)
        coef_real = jnp.sum(res_real * cosine + res_imag * sine, axis=1) * inverse[:, None]
        coef_imag = jnp.sum(res_imag * cosine - res_real * sine, axis=1) * inverse[:, None]
        mask = live[:, :, None]
        res_real = res_real - mask * (coef_real[:, None, :] * cosine - coef_imag[:, None, :] * sine)
        res_imag = res_imag - mask * (coef_real[:, None, :] * sine + coef_imag[:, None, :] * cosine)
        gathered.append(jnp.stack([coef_real, coef_imag], axis=1))
    rounded = jnp.concatenate([res_real, res_imag], axis=2).astype(jnp.bfloat16)
    spectrum = lax.map(one_patch, (rounded, jnp.moveaxis(coords, 1, 0), jnp.moveaxis(wavenumbers, 1, 0)))
    spectrum = jnp.moveaxis(spectrum, 0, 1)
    return (spectrum, jnp.stack(gathered, axis=0))
```

```python
import functools
import math

import jax
import jax.numpy as jnp
import ml_dtypes
import numpy as np
from jax import lax
from jax.experimental import pallas as pl
from jax.experimental.pallas import tpu as pltpu
from jax.sharding import PartitionSpec as P

NF = 1024
DIGIT = 32
ITERS = 2
PRE = 4
MESH = pl.DeviceIdType.MESH

SIN_ATOM = (6.2830558, -41.33121428, 81.36681487, -74.47800194, 32.78139554)
COS_ATOM = (0.9999598, -19.73104175, 64.6734317, -82.40355228, 45.64655792)
SIN_FINE = (6.28318527, -41.34169707, 81.60502462, -76.70155117, 42.01616576, -14.86861079, 3.19969338)
COS_FINE = (0.99999999, -19.73920453, 64.93911899, -85.45016556, 60.16783179, -25.96831339, 6.52961042)


def horner(u, coefs):
    acc = u * coefs[-1] + coefs[-2]
    for c in coefs[-3::-1]:
        acc = acc * u + c
    return acc


def turn(x, sin_coefs, cos_coefs):
    x = x - jnp.round(x)
    u = x * x
    return horner(u, cos_coefs), horner(u, sin_coefs) * x


def dft_blocks(length, blocks):
    sample = np.arange(length, dtype=np.int64)
    bins = np.arange(NF, dtype=np.int64)
    angle = (sample[:, None] * bins[None, :] % length) * (2.0 * math.pi / length)
    pair = np.stack([np.cos(angle), -np.sin(angle)], axis=1).astype(np.float32)
    width = NF // blocks
    pair = pair.reshape(length, 2, blocks, width).transpose(2, 0, 1, 3)
    return pair.reshape(blocks, length, 2 * width).astype(ml_dtypes.bfloat16)


def kernel(n_freq, n_trace, traces, table, wd, cd, cdt, kd, live, inv, recv, coef_out,
           tab, spec, spread, osc, res, atoms, obuf, coef_my,
           tab_sem, s_send, s_recv, s_loc, c_send, c_recv, o_send, o_recv, o_loc):
    halves = n_trace // n_freq
    g = lax.axis_index("freq")
    t = lax.axis_index("trace")
    own_patch = t // halves
    slots = spread.shape[1]
    total = n_trace * slots
    fb = osc.shape[2]
    share = obuf.shape[1]
    n_buf = atoms.shape[0]
    pre = n_buf - 1

    def table_copy(j):
        block = lax.rem(j + t, n_trace)
        return pltpu.make_async_copy(table.at[block], tab.at[lax.rem(j, 2)], tab_sem.at[lax.rem(j, 2)])

    table_copy(0).start()

    barrier = pltpu.get_barrier_semaphore()

    @pl.loop(0, n_trace)
    def _(k):
        @pl.when(jnp.logical_or(own_patch != g, k != t))
        def _():
            pl.semaphore_signal(barrier, inc=1, device_id=(own_patch, k), device_id_type=MESH)

        @pl.when(k != t)
        def _():
            pl.semaphore_signal(barrier, inc=1, device_id=(g, k), device_id_type=MESH)

    pl.semaphore_wait(barrier, 2 * n_trace - 1 - (own_patch == g).astype(jnp.int32))

    def spec_copy(j):
        block = lax.rem(j + t, n_trace)
        to_freq, to_trace = block // halves, g * halves + lax.rem(block, halves)
        return to_freq, to_trace, pltpu.make_async_remote_copy(
            src_ref=spec.at[j], dst_ref=spread.at[t], send_sem=s_send.at[j], recv_sem=s_recv.at[t],
            device_id=(to_freq, to_trace), device_id_type=MESH)

    def self_copy(j):
        return pltpu.make_async_copy(spec.at[j], spread.at[t], s_loc)

    @pl.loop(0, n_trace)
    def _(j):
        @pl.when(j + 1 < n_trace)
        def _():
            table_copy(j + 1).start()

        table_copy(j).wait()
        spec[j] = jnp.dot(traces[...], tab[lax.rem(j, 2)], preferred_element_type=jnp.float32).astype(jnp.bfloat16)
        to_freq, to_trace, copy = spec_copy(j)
        mine = jnp.logical_and(to_freq == g, to_trace == t)

        @pl.when(mine)
        def _():
            self_copy(j).start()

        @pl.when(jnp.logical_not(mine))
        def _():
            copy.start()

    rows = min(256, share)
    lanes = 256

    def make_atoms(i):
        base = lax.rem(t + 1 + i, n_trace) * share
        buf = lax.rem(i, n_buf)

        @pl.loop(0, (share // rows) * (total // lanes))
        def _(q):
            r = pl.multiple_of((q // (total // lanes)) * rows, rows)
            c = pl.multiple_of(lax.rem(q, total // lanes) * lanes, lanes)
            x = jnp.dot(wd[pl.ds(base + r, rows), :], cd[:, pl.ds(c, lanes)], preferred_element_type=jnp.float32)
            cosine, sine = turn(x, SIN_ATOM, COS_ATOM)
            atoms[buf, pl.ds(r, rows), pl.ds(c, lanes)] = cosine.astype(jnp.bfloat16)
            atoms[buf, pl.ds(r, rows), pl.ds(total + c, lanes)] = sine.astype(jnp.bfloat16)

    @pl.loop(0, n_trace)
    def _(k):
        at = pl.ds(pl.multiple_of(k * slots, slots), slots)
        on = live[at, :]
        for it in range(ITERS):
            x = jnp.dot(cdt[at, :], kd[it], preferred_element_type=jnp.float32)
            cosine, sine = turn(x, SIN_FINE, COS_FINE)
            osc[2 * it, at, :] = cosine * on
            osc[2 * it + 1, at, :] = sine * on

    @pl.loop(0, pre)
    def _(i):
        make_atoms(i)

    def fold8(a):
        return jnp.sum(a.reshape(a.shape[0] // 8, 8, fb), axis=0)

    def add_block(k, sums):
        own = jnp.logical_and(own_patch == g, k == t)

        @pl.when(own)
        def _():
            pltpu.make_async_copy(spec.at[0], spread.at[k], s_loc).wait()

        @pl.when(jnp.logical_not(own))
        def _():
            pltpu.make_async_remote_copy(
                src_ref=spec.at[0], dst_ref=spread.at[k], send_sem=s_send.at[0], recv_sem=s_recv.at[k],
                device_id=(own_patch, k), device_id_type=MESH).wait_recv()

        at = pl.ds(pl.multiple_of(k * slots, slots), slots)
        x = spread[k].astype(jnp.float32)
        re, im = x[:, :fb], x[:, fb:]
        c1, s1, c2, s2 = (osc[n, at, :] for n in range(4))
        terms = (re * c1 + im * s1, im * c1 - re * s1, re * c2 + im * s2, im * c2 - re * s2,
                 c1 * c2 + s1 * s2, s1 * c2 - c1 * s2)
        return tuple(a + fold8(b) for a, b in zip(sums, terms))

    zero = jnp.zeros((8, fb), jnp.float32)
    sums = lax.fori_loop(0, n_trace, add_block, (zero,) * 6)
    p1r, p1i, p2r, p2i, gr, gi = (jnp.sum(a, axis=0, keepdims=True) for a in sums)
    scale = inv[...]
    a1r, a1i = p1r * scale, p1i * scale
    a2r = (p2r - (a1r * gr - a1i * gi)) * scale
    a2i = (p2i - (a1r * gi + a1i * gr)) * scale
    coef_my[...] = jnp.zeros_like(coef_my)
    for n, a in enumerate((a1r, a1i, a2r, a2i)):
        coef_my[n : n + 1, :] = a

    def coef_copy(k):
        return pltpu.make_async_remote_copy(
            src_ref=coef_my, dst_ref=coef_out.at[t], send_sem=c_send.at[k], recv_sem=c_recv.at[t],
            device_id=(g, k), device_id_type=MESH)

    @pl.loop(0, n_trace)
    def _(k):
        @pl.when(k != t)
        def _():
            coef_copy(k).start()

        @pl.when(k == t)
        def _():
            coef_out[t] = coef_my[...]

    @pl.loop(0, n_trace)
    def _(k):
        at = pl.ds(pl.multiple_of(k * slots, slots), slots)
        under = pl.ds(pl.multiple_of(total + k * slots, slots), slots)
        on = live[at, :]
        x = spread[k].astype(jnp.float32)
        c1, s1, c2, s2 = (osc[n, at, :] for n in range(4))
        re = x[:, :fb] * on - (a1r * c1 - a1i * s1) - (a2r * c2 - a2i * s2)
        im = x[:, fb:] * on - (a1r * s1 + a1i * c1) - (a2r * s2 + a2i * c2)
        res[at, :fb] = re.astype(jnp.bfloat16)
        res[at, fb:] = im.astype(jnp.bfloat16)
        res[under, :fb] = im.astype(jnp.bfloat16)
        res[under, fb:] = (-re).astype(jnp.bfloat16)

    def out_copy(i):
        return pltpu.make_async_remote_copy(
            src_ref=obuf.at[i], dst_ref=recv.at[t], send_sem=o_send.at[i], recv_sem=o_recv.at[t],
            device_id=(g, lax.rem(t + 1 + i, n_trace)), device_id_type=MESH)

    @pl.loop(0, n_trace)
    def _(i):
        buf = lax.rem(i, n_buf)

        @pl.loop(0, share // rows)
        def _(r):
            at = pl.ds(pl.multiple_of(r * rows, rows), rows)
            obuf[i, at, :] = jnp.dot(atoms[buf, at, :], res[...], preferred_element_type=jnp.float32).astype(jnp.bfloat16)

        @pl.when(i < n_trace - 1)
        def _():
            out_copy(i).start()

        @pl.when(i + pre < n_trace)
        def _():
            make_atoms(i + pre)

    own_out = pltpu.make_async_copy(obuf.at[n_trace - 1], recv.at[t], o_loc)
    own_out.start()

    @pl.loop(0, n_trace)
    def _(j):
        to_freq, to_trace, copy = spec_copy(j)

        @pl.when(jnp.logical_not(jnp.logical_and(to_freq == g, to_trace == t)))
        def _():
            copy.wait_send()

        @pl.when(j != t)
        def _():
            coef_copy(j).wait_send()
            pltpu.make_async_remote_copy(
                src_ref=coef_my, dst_ref=coef_out.at[j], send_sem=c_send.at[j], recv_sem=c_recv.at[j],
                device_id=(g, j), device_id_type=MESH).wait_recv()
            pltpu.make_async_remote_copy(
                src_ref=obuf.at[0], dst_ref=recv.at[j], send_sem=o_send.at[0], recv_sem=o_recv.at[j],
                device_id=(g, j), device_id_type=MESH).wait_recv()

        @pl.when(j < n_trace - 1)
        def _():
            out_copy(j).wait_send()

    own_out.wait()


def digits_low(v):
    a, b = v // DIGIT, v % DIGIT
    rows = jnp.concatenate([a * DIGIT, b * DIGIT, b], axis=0).astype(jnp.float32) / (DIGIT * DIGIT)
    return jnp.pad(rows, ((0, 4), (0, 0))).astype(jnp.bfloat16)


def digits_high(v):
    d, e = v // DIGIT, v % DIGIT
    rows = jnp.concatenate([e, d, e], axis=0)
    return jnp.pad(rows, ((0, 4), (0, 0))).astype(jnp.bfloat16)


def local(traces, coords, wavenumbers, fold, selected):
    slots, length = traces.shape[1:]
    n_freq, n_trace = lax.axis_size("freq"), lax.axis_size("trace")
    patches = coords.shape[1]
    halves = n_trace // n_freq
    fb = NF // n_trace
    n_waves = wavenumbers.shape[2]
    share = n_waves // n_trace
    total = coords.shape[2]
    t = lax.axis_index("trace")
    patch = t // halves
    table = jnp.asarray(dft_blocks(length, n_trace))
    waves = digits_low(lax.dynamic_index_in_dim(wavenumbers, patch, 1, keepdims=False))
    places = digits_high(lax.dynamic_index_in_dim(coords, patch, 1, keepdims=False))
    chosen = lax.dynamic_slice(selected, (0, patch, lax.rem(t, halves) * fb), (ITERS, 1, fb)).reshape(-1)
    onehot = (jnp.arange(n_waves, dtype=jnp.int32)[:, None] == chosen[None, :]).astype(jnp.bfloat16)
    picked = jnp.dot(waves, onehot, preferred_element_type=jnp.float32).astype(jnp.bfloat16)
    kd = picked.reshape(16, ITERS, fb).transpose(1, 0, 2)
    my_fold = lax.dynamic_index_in_dim(fold, patch, 0, keepdims=False)
    live = (jnp.arange(total, dtype=jnp.int32) < my_fold).astype(jnp.float32)
    live = jnp.broadcast_to(live[:, None], (total, fb))
    inv = jnp.broadcast_to(1.0 / my_fold.astype(jnp.float32), (1, fb))
    vmem = pl.BlockSpec(memory_space=pltpu.VMEM)
    hbm = pl.BlockSpec(memory_space=pl.ANY)
    dma = pltpu.SemaphoreType.DMA
    n_buf = min(PRE, n_trace - 1) + 1
    bf16, f32 = jnp.bfloat16, jnp.float32
    recv, coef = pl.pallas_call(
        functools.partial(kernel, n_freq, n_trace),
        out_shape=(jax.ShapeDtypeStruct((n_trace, share, 2 * fb), bf16),
                   jax.ShapeDtypeStruct((n_trace, 8, fb), f32)),
        in_specs=[vmem, hbm, vmem, vmem, vmem, vmem, vmem, vmem],
        out_specs=(hbm, vmem),
        scratch_shapes=[
            pltpu.VMEM((2, length, 2 * fb), bf16),
            pltpu.VMEM((n_trace, slots, 2 * fb), bf16),
            pltpu.VMEM((n_trace, slots, 2 * fb), bf16),
            pltpu.VMEM((2 * ITERS, total, fb), f32),
            pltpu.VMEM((2 * total, 2 * fb), bf16),
            pltpu.VMEM((n_buf, share, 2 * total), bf16),
            pltpu.VMEM((n_trace, share, 2 * fb), bf16),
            pltpu.VMEM((8, fb), f32),
            dma((2,)), dma((n_trace,)), dma((n_trace,)), dma,
            dma((n_trace,)), dma((n_trace,)), dma((n_trace,)), dma((n_trace,)), dma,
        ],
        compiler_params=pltpu.CompilerParams(
            collective_id=0, has_side_effects=True, vmem_limit_bytes=58 * 1024 * 1024),
    )(traces[0], table, waves.T, places, places.T, kd, live, inv)
    spectrum = recv.reshape(patches, halves, share, 2, fb).transpose(2, 0, 3, 1, 4)
    spectrum = spectrum.reshape(share, patches, 2, halves * fb).astype(f32)
    coef = coef[:, : 2 * ITERS].reshape(patches, halves, ITERS, 2, fb).transpose(2, 0, 3, 1, 4)
    return spectrum, coef.reshape(ITERS, patches, 2, halves * fb)


def solution(mesh):
    in_specs = (P("freq", "trace", None), P(), P(), P(), P(None, None, "freq"))
    out_specs = (P("trace", None, None, "freq"), P(None, None, None, "freq"))
    return jax.shard_map(local, mesh=mesh, in_specs=in_specs, out_specs=out_specs, check_vma=False)
```

```python
import functools
import math

import jax
import jax.numpy as jnp
import ml_dtypes
import numpy as np
from jax import lax
from jax.experimental import pallas as pl
from jax.experimental.pallas import tpu as pltpu
from jax.sharding import PartitionSpec as P

NF = 1024
DIGIT = 32
ITERS = 2
PRE = 4
MESH = pl.DeviceIdType.MESH

SIN_ATOM = (6.2830558, -41.33121428, 81.36681487, -74.47800194, 32.78139554)
COS_ATOM = (0.9999598, -19.73104175, 64.6734317, -82.40355228, 45.64655792)
SIN_FINE = (6.28318527, -41.34169707, 81.60502462, -76.70155117, 42.01616576, -14.86861079, 3.19969338)
COS_FINE = (0.99999999, -19.73920453, 64.93911899, -85.45016556, 60.16783179, -25.96831339, 6.52961042)


def horner(u, coefs):
    acc = u * coefs[-1] + coefs[-2]
    for c in coefs[-3::-1]:
        acc = acc * u + c
    return acc


def turn(x, sin_coefs, cos_coefs):
    x = x - jnp.round(x)
    u = x * x
    return horner(u, cos_coefs), horner(u, sin_coefs) * x


def dft_blocks(length, blocks):
    sample = np.arange(length, dtype=np.int64)
    bins = np.arange(NF, dtype=np.int64)
    angle = (sample[:, None] * bins[None, :] % length) * (2.0 * math.pi / length)
    pair = np.stack([np.cos(angle), -np.sin(angle)], axis=1).astype(np.float32)
    width = NF // blocks
    pair = pair.reshape(length, 2, blocks, width).transpose(2, 0, 1, 3)
    return pair.reshape(blocks, length, 2 * width).astype(ml_dtypes.bfloat16)


def kernel(n_freq, n_trace, traces, table, wd, cd, cdt, kd, live, inv, recv, coef_out,
           tab, spec, spread, osc, res, atoms, obuf, coef_my,
           tab_sem, s_send, s_recv, s_loc, c_send, c_recv, o_send, o_recv, o_loc):
    halves = n_trace // n_freq
    g = lax.axis_index("freq")
    t = lax.axis_index("trace")
    own_patch = lax.rem(t // halves + g, n_freq)
    slots = spread.shape[1]
    total = n_trace * slots
    fb = osc.shape[2]
    share = obuf.shape[1]
    n_buf = atoms.shape[0]
    pre = n_buf - 1

    def table_copy(j):
        block = lax.rem(j + t, n_trace)
        return pltpu.make_async_copy(table.at[block], tab.at[lax.rem(j, 2)], tab_sem.at[lax.rem(j, 2)])

    table_copy(0).start()

    barrier = pltpu.get_barrier_semaphore()

    @pl.loop(0, n_trace)
    def _(k):
        @pl.when(jnp.logical_or(own_patch != g, k != t))
        def _():
            pl.semaphore_signal(barrier, inc=1, device_id=(own_patch, k), device_id_type=MESH)

        @pl.when(k != t)
        def _():
            pl.semaphore_signal(barrier, inc=1, device_id=(g, k), device_id_type=MESH)

    pl.semaphore_wait(barrier, 2 * n_trace - 1 - (own_patch == g).astype(jnp.int32))

    def spec_copy(j):
        block = lax.rem(j + t, n_trace)
        to_freq = block // halves
        to_trace = lax.rem(g + n_freq - to_freq, n_freq) * halves + lax.rem(block, halves)
        return to_freq, to_trace, pltpu.make_async_remote_copy(
            src_ref=spec.at[j], dst_ref=spread.at[t], send_sem=s_send.at[j], recv_sem=s_recv.at[t],
            device_id=(to_freq, to_trace), device_id_type=MESH)

    def self_copy(j):
        return pltpu.make_async_copy(spec.at[j], spread.at[t], s_loc)

    @pl.loop(0, n_trace)
    def _(j):
        @pl.when(j + 1 < n_trace)
        def _():
            table_copy(j + 1).start()

        table_copy(j).wait()
        spec[j] = jnp.dot(traces[...], tab[lax.rem(j, 2)], preferred_element_type=jnp.float32).astype(jnp.bfloat16)
        to_freq, to_trace, copy = spec_copy(j)
        mine = jnp.logical_and(to_freq == g, to_trace == t)

        @pl.when(mine)
        def _():
            self_copy(j).start()

        @pl.when(jnp.logical_not(mine))
        def _():
            copy.start()

    rows = min(256, share)
    lanes = 256

    def make_atoms(i):
        base = lax.rem(t + 1 + i, n_trace) * share
        buf = lax.rem(i, n_buf)

        @pl.loop(0, (share // rows) * (total // lanes))
        def _(q):
            r = pl.multiple_of((q // (total // lanes)) * rows, rows)
            c = pl.multiple_of(lax.rem(q, total // lanes) * lanes, lanes)
            x = jnp.dot(wd[pl.ds(base + r, rows), :], cd[:, pl.ds(c, lanes)], preferred_element_type=jnp.float32)
            cosine, sine = turn(x, SIN_ATOM, COS_ATOM)
            atoms[buf, pl.ds(r, rows), pl.ds(c, lanes)] = cosine.astype(jnp.bfloat16)
            atoms[buf, pl.ds(r, rows), pl.ds(total + c, lanes)] = sine.astype(jnp.bfloat16)

    @pl.loop(0, n_trace)
    def _(k):
        at = pl.ds(pl.multiple_of(k * slots, slots), slots)
        on = live[at, :]
        for it in range(ITERS):
            x = jnp.dot(cdt[at, :], kd[it], preferred_element_type=jnp.float32)
            cosine, sine = turn(x, SIN_FINE, COS_FINE)
            osc[2 * it, at, :] = cosine * on
            osc[2 * it + 1, at, :] = sine * on

    @pl.loop(0, pre)
    def _(i):
        make_atoms(i)

    def fold8(a):
        return jnp.sum(a.reshape(a.shape[0] // 8, 8, fb), axis=0)

    def add_block(k, sums):
        own = jnp.logical_and(own_patch == g, k == t)

        @pl.when(own)
        def _():
            pltpu.make_async_copy(spec.at[0], spread.at[k], s_loc).wait()

        @pl.when(jnp.logical_not(own))
        def _():
            pltpu.make_async_remote_copy(
                src_ref=spec.at[0], dst_ref=spread.at[k], send_sem=s_send.at[0], recv_sem=s_recv.at[k],
                device_id=(own_patch, k), device_id_type=MESH).wait_recv()

        at = pl.ds(pl.multiple_of(k * slots, slots), slots)
        x = spread[k].astype(jnp.float32)
        re, im = x[:, :fb], x[:, fb:]
        c1, s1, c2, s2 = (osc[n, at, :] for n in range(4))
        terms = (re * c1 + im * s1, im * c1 - re * s1, re * c2 + im * s2, im * c2 - re * s2,
                 c1 * c2 + s1 * s2, s1 * c2 - c1 * s2)
        return tuple(a + fold8(b) for a, b in zip(sums, terms))

    zero = jnp.zeros((8, fb), jnp.float32)
    sums = lax.fori_loop(0, n_trace, add_block, (zero,) * 6)
    p1r, p1i, p2r, p2i, gr, gi = (jnp.sum(a, axis=0, keepdims=True) for a in sums)
    scale = inv[...]
    a1r, a1i = p1r * scale, p1i * scale
    a2r = (p2r - (a1r * gr - a1i * gi)) * scale
    a2i = (p2i - (a1r * gi + a1i * gr)) * scale
    coef_my[...] = jnp.zeros_like(coef_my)
    for n, a in enumerate((a1r, a1i, a2r, a2i)):
        coef_my[n : n + 1, :] = a

    def coef_copy(k):
        return pltpu.make_async_remote_copy(
            src_ref=coef_my, dst_ref=coef_out.at[t], send_sem=c_send.at[k], recv_sem=c_recv.at[t],
            device_id=(g, k), device_id_type=MESH)

    @pl.loop(0, n_trace)
    def _(k):
        @pl.when(k != t)
        def _():
            coef_copy(k).start()

        @pl.when(k == t)
        def _():
            coef_out[t] = coef_my[...]

    @pl.loop(0, n_trace)
    def _(k):
        at = pl.ds(pl.multiple_of(k * slots, slots), slots)
        under = pl.ds(pl.multiple_of(total + k * slots, slots), slots)
        on = live[at, :]
        x = spread[k].astype(jnp.float32)
        c1, s1, c2, s2 = (osc[n, at, :] for n in range(4))
        re = x[:, :fb] * on - (a1r * c1 - a1i * s1) - (a2r * c2 - a2i * s2)
        im = x[:, fb:] * on - (a1r * s1 + a1i * c1) - (a2r * s2 + a2i * c2)
        res[at, :fb] = re.astype(jnp.bfloat16)
        res[at, fb:] = im.astype(jnp.bfloat16)
        res[under, :fb] = im.astype(jnp.bfloat16)
        res[under, fb:] = (-re).astype(jnp.bfloat16)

    def out_copy(i):
        return pltpu.make_async_remote_copy(
            src_ref=obuf.at[i], dst_ref=recv.at[t], send_sem=o_send.at[i], recv_sem=o_recv.at[t],
            device_id=(g, lax.rem(t + 1 + i, n_trace)), device_id_type=MESH)

    @pl.loop(0, n_trace)
    def _(i):
        buf = lax.rem(i, n_buf)

        @pl.loop(0, share // rows)
        def _(r):
            at = pl.ds(pl.multiple_of(r * rows, rows), rows)
            obuf[i, at, :] = jnp.dot(atoms[buf, at, :], res[...], preferred_element_type=jnp.float32).astype(jnp.bfloat16)

        @pl.when(i < n_trace - 1)
        def _():
            out_copy(i).start()

        @pl.when(i + pre < n_trace)
        def _():
            make_atoms(i + pre)

    own_out = pltpu.make_async_copy(obuf.at[n_trace - 1], recv.at[t], o_loc)
    own_out.start()

    @pl.loop(0, n_trace)
    def _(j):
        to_freq, to_trace, copy = spec_copy(j)

        @pl.when(jnp.logical_not(jnp.logical_and(to_freq == g, to_trace == t)))
        def _():
            copy.wait_send()

        @pl.when(j != t)
        def _():
            coef_copy(j).wait_send()
            pltpu.make_async_remote_copy(
                src_ref=coef_my, dst_ref=coef_out.at[j], send_sem=c_send.at[j], recv_sem=c_recv.at[j],
                device_id=(g, j), device_id_type=MESH).wait_recv()
            pltpu.make_async_remote_copy(
                src_ref=obuf.at[0], dst_ref=recv.at[j], send_sem=o_send.at[0], recv_sem=o_recv.at[j],
                device_id=(g, j), device_id_type=MESH).wait_recv()

        @pl.when(j < n_trace - 1)
        def _():
            out_copy(j).wait_send()

    own_out.wait()


def unpack(patches, recv, out):
    n_trace, step, _ = recv.shape
    halves = n_trace // patches
    fb = recv.shape[2] // 2
    row = out.shape[1]
    blocks = halves * fb // row
    stride = patches * blocks * 2
    g = lax.axis_index("freq")
    for p in range(patches):
        at = lax.rem(p + patches - g, patches) * halves
        parts = [recv[at + h].astype(jnp.float32) for h in range(halves)]
        for ri in range(2):
            full = jnp.concatenate([a[:, ri * fb : (ri + 1) * fb] for a in parts], axis=1)
            for b in range(blocks):
                first = (p * blocks + b) * 2 + ri
                out[pl.ds(first, step, stride=stride), :] = full[:, b * row : (b + 1) * row]


def digits_low(v):
    a, b = v // DIGIT, v % DIGIT
    rows = jnp.concatenate([a * DIGIT, b * DIGIT, b], axis=0).astype(jnp.float32) / (DIGIT * DIGIT)
    return jnp.pad(rows, ((0, 4), (0, 0))).astype(jnp.bfloat16)


def digits_high(v):
    d, e = v // DIGIT, v % DIGIT
    rows = jnp.concatenate([e, d, e], axis=0)
    return jnp.pad(rows, ((0, 4), (0, 0))).astype(jnp.bfloat16)


def local(traces, coords, wavenumbers, fold, selected):
    slots, length = traces.shape[1:]
    n_freq, n_trace = lax.axis_size("freq"), lax.axis_size("trace")
    patches = coords.shape[1]
    halves = n_trace // n_freq
    fb = NF // n_trace
    n_waves = wavenumbers.shape[2]
    share = n_waves // n_trace
    total = coords.shape[2]
    t = lax.axis_index("trace")
    patch = lax.rem(t // halves + lax.axis_index("freq"), patches)
    table = jnp.asarray(dft_blocks(length, n_trace))
    waves = digits_low(lax.dynamic_index_in_dim(wavenumbers, patch, 1, keepdims=False))
    places = digits_high(lax.dynamic_index_in_dim(coords, patch, 1, keepdims=False))
    chosen = lax.dynamic_slice(selected, (0, patch, lax.rem(t, halves) * fb), (ITERS, 1, fb)).reshape(-1)
    onehot = (jnp.arange(n_waves, dtype=jnp.int32)[:, None] == chosen[None, :]).astype(jnp.bfloat16)
    picked = jnp.dot(waves, onehot, preferred_element_type=jnp.float32).astype(jnp.bfloat16)
    kd = picked.reshape(16, ITERS, fb).transpose(1, 0, 2)
    my_fold = lax.dynamic_index_in_dim(fold, patch, 0, keepdims=False)
    live = (jnp.arange(total, dtype=jnp.int32) < my_fold).astype(jnp.float32)
    live = jnp.broadcast_to(live[:, None], (total, fb))
    inv = jnp.broadcast_to(1.0 / my_fold.astype(jnp.float32), (1, fb))
    vmem = pl.BlockSpec(memory_space=pltpu.VMEM)
    hbm = pl.BlockSpec(memory_space=pl.ANY)
    dma = pltpu.SemaphoreType.DMA
    n_buf = min(PRE, n_trace - 1) + 1
    bf16, f32 = jnp.bfloat16, jnp.float32
    recv, coef = pl.pallas_call(
        functools.partial(kernel, n_freq, n_trace),
        out_shape=(jax.ShapeDtypeStruct((n_trace, share, 2 * fb), bf16),
                   jax.ShapeDtypeStruct((n_trace, 8, fb), f32)),
        in_specs=[vmem, hbm, vmem, vmem, vmem, vmem, vmem, vmem],
        out_specs=(hbm, vmem),
        scratch_shapes=[
            pltpu.VMEM((2, length, 2 * fb), bf16),
            pltpu.VMEM((n_trace, slots, 2 * fb), bf16),
            pltpu.VMEM((n_trace, slots, 2 * fb), bf16),
            pltpu.VMEM((2 * ITERS, total, fb), f32),
            pltpu.VMEM((2 * total, 2 * fb), bf16),
            pltpu.VMEM((n_buf, share, 2 * total), bf16),
            pltpu.VMEM((n_trace, share, 2 * fb), bf16),
            pltpu.VMEM((8, fb), f32),
            dma((2,)), dma((n_trace,)), dma((n_trace,)), dma,
            dma((n_trace,)), dma((n_trace,)), dma((n_trace,)), dma((n_trace,)), dma,
        ],
        compiler_params=pltpu.CompilerParams(
            collective_id=0, has_side_effects=True, vmem_limit_bytes=58 * 1024 * 1024),
    )(traces[0], table, waves.T, places, places.T, kd, live, inv)
    width = halves * fb
    row = min(width, 128)
    step = min(share, 128)
    rows = patches * 2 * (width // row)
    spectrum = pl.pallas_call(
        functools.partial(unpack, patches),
        out_shape=jax.ShapeDtypeStruct((share * rows, row), f32),
        grid=(share // step,),
        in_specs=[pl.BlockSpec((n_trace, step, 2 * fb), lambda i: (0, i, 0))],
        out_specs=pl.BlockSpec((step * rows, row), lambda i: (i, 0)),
    )(recv)
    spectrum = spectrum.reshape(share, patches, width // row, 2, row).transpose(0, 1, 3, 2, 4)
    spectrum = spectrum.reshape(share, patches, 2, width)
    coef = jnp.roll(coef[:, : 2 * ITERS], halves * lax.axis_index("freq"), axis=0)
    coef = coef.reshape(patches, halves, ITERS, 2, fb).transpose(2, 0, 3, 1, 4)
    return spectrum, coef.reshape(ITERS, patches, 2, width)


def solution(mesh):
    in_specs = (P("freq", "trace", None), P(), P(), P(), P(None, None, "freq"))
    out_specs = (P("trace", None, None, "freq"), P(None, None, None, "freq"))
    return jax.shard_map(local, mesh=mesh, in_specs=in_specs, out_specs=out_specs, check_vma=False)
```

```python
import functools
import math

import jax
import jax.numpy as jnp
import ml_dtypes
import numpy as np
from jax import lax
from jax.experimental import pallas as pl
from jax.experimental.pallas import tpu as pltpu
from jax.sharding import PartitionSpec as P

NF = 1024
DIGIT = 32
ITERS = 2
PRE = 5
MESH = pl.DeviceIdType.MESH

SIN_ATOM = (6.27863545, -41.09373054, 77.93034795, -56.08638961)
ROUNDER = 12582912.0
COS_ATOM = (0.9999598, -19.73104175, 64.6734317, -82.40355228, 45.64655792)
SIN_FINE = (6.28318527, -41.34169707, 81.60502462, -76.70155117, 42.01616576, -14.86861079, 3.19969338)
COS_FINE = (0.99999999, -19.73920453, 64.93911899, -85.45016556, 60.16783179, -25.96831339, 6.52961042)


def horner(u, coefs):
    acc = u * coefs[-1] + coefs[-2]
    for c in coefs[-3::-1]:
        acc = acc * u + c
    return acc


def turn(x, sin_coefs, cos_coefs):
    x = x - ((x + ROUNDER) - ROUNDER)
    u = x * x
    return horner(u, cos_coefs), horner(u, sin_coefs) * x


def dft_blocks(length, blocks):
    sample = np.arange(length, dtype=np.int64)
    bins = np.arange(NF, dtype=np.int64)
    angle = (sample[:, None] * bins[None, :] % length) * (2.0 * math.pi / length)
    pair = np.stack([np.cos(angle), -np.sin(angle)], axis=1).astype(np.float32)
    width = NF // blocks
    pair = pair.reshape(length, 2, blocks, width).transpose(2, 0, 1, 3)
    return pair.reshape(blocks, length, 2 * width).astype(ml_dtypes.bfloat16)


def kernel(n_freq, n_trace, traces, table, wd, cd, cdt, kd, fold, recv, coef_out,
           tab, spec, spread, osc, res, atoms, obuf, coef_my,
           tab_sem, s_send, s_recv, s_loc, c_send, c_recv, o_send, o_recv, o_loc):
    halves = n_trace // n_freq
    g = lax.axis_index("freq")
    t = lax.axis_index("trace")
    own_patch = lax.rem(t // halves + g, n_freq)
    slots = spread.shape[1]
    total = n_trace * slots
    fb = osc.shape[2]
    share = obuf.shape[1]
    n_buf = atoms.shape[0]
    pre = n_buf

    def table_copy(j):
        block = lax.rem(j + t, n_trace)
        return pltpu.make_async_copy(table.at[block], tab.at[lax.rem(j, 2)], tab_sem.at[lax.rem(j, 2)])

    table_copy(0).start()

    barrier = pltpu.get_barrier_semaphore()

    @pl.loop(0, n_trace)
    def _(k):
        @pl.when(jnp.logical_or(own_patch != g, k != t))
        def _():
            pl.semaphore_signal(barrier, inc=1, device_id=(own_patch, k), device_id_type=MESH)

        @pl.when(k != t)
        def _():
            pl.semaphore_signal(barrier, inc=1, device_id=(g, k), device_id_type=MESH)

    pl.semaphore_wait(barrier, 2 * n_trace - 1 - (own_patch == g).astype(jnp.int32))

    def spec_copy(j):
        block = lax.rem(j + t, n_trace)
        to_freq = block // halves
        to_trace = lax.rem(g + n_freq - to_freq, n_freq) * halves + lax.rem(block, halves)
        return to_freq, to_trace, pltpu.make_async_remote_copy(
            src_ref=spec.at[j], dst_ref=spread.at[t], send_sem=s_send.at[j], recv_sem=s_recv.at[t],
            device_id=(to_freq, to_trace), device_id_type=MESH)

    def self_copy(j):
        return pltpu.make_async_copy(spec.at[j], spread.at[t], s_loc)

    @pl.loop(0, n_trace)
    def _(j):
        @pl.when(j + 1 < n_trace)
        def _():
            table_copy(j + 1).start()

        table_copy(j).wait()
        spec[j] = jnp.dot(traces[...], tab[lax.rem(j, 2)], preferred_element_type=jnp.float32).astype(jnp.bfloat16)
        to_freq, to_trace, copy = spec_copy(j)
        mine = jnp.logical_and(to_freq == g, to_trace == t)

        @pl.when(mine)
        def _():
            self_copy(j).start()

        @pl.when(jnp.logical_not(mine))
        def _():
            copy.start()

    def live(k):
        slot = lax.broadcasted_iota(jnp.int32, (slots, fb), 0) + k * slots
        return jnp.where(slot.astype(jnp.float32) < fold[...], 1.0, 0.0)

    rows = min(256, share)
    lanes = 256

    def make_atoms(i):
        base = lax.rem(t + 1 + i, n_trace) * share
        buf = lax.rem(i, n_buf)

        @pl.loop(0, (share // rows) * (total // lanes))
        def _(q):
            r = pl.multiple_of((q // (total // lanes)) * rows, rows)
            c = pl.multiple_of(lax.rem(q, total // lanes) * lanes, lanes)
            x = jnp.dot(wd[pl.ds(base + r, rows), :], cd[:, pl.ds(c, lanes)], preferred_element_type=jnp.float32)
            cosine, sine = turn(x, SIN_ATOM, COS_ATOM)
            atoms[buf, pl.ds(r, rows), pl.ds(c, lanes)] = cosine.astype(jnp.bfloat16)
            atoms[buf, pl.ds(r, rows), pl.ds(total + c, lanes)] = sine.astype(jnp.bfloat16)

    @pl.loop(0, n_trace)
    def _(k):
        at = pl.ds(pl.multiple_of(k * slots, slots), slots)
        on = live(k)
        for it in range(ITERS):
            x = jnp.dot(cdt[at, :], kd[it], preferred_element_type=jnp.float32)
            cosine, sine = turn(x, SIN_FINE, COS_FINE)
            osc[2 * it, at, :] = cosine * on
            osc[2 * it + 1, at, :] = sine * on

    @pl.loop(0, pre)
    def _(i):
        make_atoms(i)

    def fold8(a):
        return jnp.sum(a.reshape(a.shape[0] // 8, 8, fb), axis=0)

    def add_block(k, sums):
        own = jnp.logical_and(own_patch == g, k == t)

        @pl.when(own)
        def _():
            pltpu.make_async_copy(spec.at[0], spread.at[k], s_loc).wait()

        @pl.when(jnp.logical_not(own))
        def _():
            pltpu.make_async_remote_copy(
                src_ref=spec.at[0], dst_ref=spread.at[k], send_sem=s_send.at[0], recv_sem=s_recv.at[k],
                device_id=(own_patch, k), device_id_type=MESH).wait_recv()

        at = pl.ds(pl.multiple_of(k * slots, slots), slots)
        x = spread[k].astype(jnp.float32)
        re, im = x[:, :fb], x[:, fb:]
        c1, s1, c2, s2 = (osc[n, at, :] for n in range(4))
        terms = (re * c1 + im * s1, im * c1 - re * s1, re * c2 + im * s2, im * c2 - re * s2,
                 c1 * c2 + s1 * s2, s1 * c2 - c1 * s2)
        return tuple(a + fold8(b) for a, b in zip(sums, terms))

    zero = jnp.zeros((8, fb), jnp.float32)
    sums = lax.fori_loop(0, n_trace, add_block, (zero,) * 6)
    p1r, p1i, p2r, p2i, gr, gi = (jnp.sum(a, axis=0, keepdims=True) for a in sums)
    scale = 1.0 / fold[...]
    a1r, a1i = p1r * scale, p1i * scale
    a2r = (p2r - (a1r * gr - a1i * gi)) * scale
    a2i = (p2i - (a1r * gi + a1i * gr)) * scale
    coef_my[...] = jnp.zeros_like(coef_my)
    for n, a in enumerate((a1r, a1i, a2r, a2i)):
        coef_my[n : n + 1, :] = a

    def coef_copy(k):
        return pltpu.make_async_remote_copy(
            src_ref=coef_my, dst_ref=coef_out.at[t], send_sem=c_send.at[k], recv_sem=c_recv.at[t],
            device_id=(g, k), device_id_type=MESH)

    @pl.loop(0, n_trace)
    def _(k):
        @pl.when(k != t)
        def _():
            coef_copy(k).start()

        @pl.when(k == t)
        def _():
            coef_out[t] = coef_my[...]

    @pl.loop(0, n_trace)
    def _(k):
        at = pl.ds(pl.multiple_of(k * slots, slots), slots)
        under = pl.ds(pl.multiple_of(total + k * slots, slots), slots)
        on = live(k)
        x = spread[k].astype(jnp.float32)
        c1, s1, c2, s2 = (osc[n, at, :] for n in range(4))
        re = x[:, :fb] * on - (a1r * c1 - a1i * s1) - (a2r * c2 - a2i * s2)
        im = x[:, fb:] * on - (a1r * s1 + a1i * c1) - (a2r * s2 + a2i * c2)
        res[at, :fb] = re.astype(jnp.bfloat16)
        res[at, fb:] = im.astype(jnp.bfloat16)
        res[under, :fb] = im.astype(jnp.bfloat16)
        res[under, fb:] = (-re).astype(jnp.bfloat16)

    def out_copy(i):
        return pltpu.make_async_remote_copy(
            src_ref=obuf.at[i], dst_ref=recv.at[t], send_sem=o_send.at[i], recv_sem=o_recv.at[t],
            device_id=(g, lax.rem(t + 1 + i, n_trace)), device_id_type=MESH)

    @pl.loop(0, n_trace)
    def _(i):
        buf = lax.rem(i, n_buf)

        @pl.when(i >= pre)
        def _():
            make_atoms(i)

        @pl.loop(0, share // rows)
        def _(r):
            at = pl.ds(pl.multiple_of(r * rows, rows), rows)
            obuf[i, at, :] = jnp.dot(atoms[buf, at, :], res[...], preferred_element_type=jnp.float32).astype(jnp.bfloat16)

        @pl.when(i < n_trace - 1)
        def _():
            out_copy(i).start()

    own_out = pltpu.make_async_copy(obuf.at[n_trace - 1], recv.at[t], o_loc)
    own_out.start()

    @pl.loop(0, n_trace)
    def _(j):
        to_freq, to_trace, copy = spec_copy(j)

        @pl.when(jnp.logical_not(jnp.logical_and(to_freq == g, to_trace == t)))
        def _():
            copy.wait_send()

        @pl.when(j != t)
        def _():
            coef_copy(j).wait_send()
            pltpu.make_async_remote_copy(
                src_ref=coef_my, dst_ref=coef_out.at[j], send_sem=c_send.at[j], recv_sem=c_recv.at[j],
                device_id=(g, j), device_id_type=MESH).wait_recv()
            pltpu.make_async_remote_copy(
                src_ref=obuf.at[0], dst_ref=recv.at[j], send_sem=o_send.at[0], recv_sem=o_recv.at[j],
                device_id=(g, j), device_id_type=MESH).wait_recv()

        @pl.when(j < n_trace - 1)
        def _():
            out_copy(j).wait_send()

    own_out.wait()


def unpack(patches, recv, out):
    n_trace, step, _ = recv.shape
    halves = n_trace // patches
    fb = recv.shape[2] // 2
    row = out.shape[1]
    blocks = halves * fb // row
    stride = patches * blocks * 2
    g = lax.axis_index("freq")
    for p in range(patches):
        at = lax.rem(p + patches - g, patches) * halves
        parts = [recv[at + h].astype(jnp.float32) for h in range(halves)]
        for ri in range(2):
            full = jnp.concatenate([a[:, ri * fb : (ri + 1) * fb] for a in parts], axis=1)
            for b in range(blocks):
                first = (p * blocks + b) * 2 + ri
                out[pl.ds(first, step, stride=stride), :] = full[:, b * row : (b + 1) * row]


def digits_low(v):
    a, b = v // DIGIT, v % DIGIT
    rows = jnp.concatenate([a * DIGIT, b * DIGIT, b], axis=0).astype(jnp.float32) / (DIGIT * DIGIT)
    return jnp.pad(rows, ((0, 4), (0, 0))).astype(jnp.bfloat16)


def digits_high(v):
    d, e = v // DIGIT, v % DIGIT
    rows = jnp.concatenate([e, d, e], axis=0)
    return jnp.pad(rows, ((0, 4), (0, 0))).astype(jnp.bfloat16)


def local(traces, coords, wavenumbers, fold, selected):
    slots, length = traces.shape[1:]
    n_freq, n_trace = lax.axis_size("freq"), lax.axis_size("trace")
    patches = coords.shape[1]
    halves = n_trace // n_freq
    fb = NF // n_trace
    n_waves = wavenumbers.shape[2]
    share = n_waves // n_trace
    total = coords.shape[2]
    t = lax.axis_index("trace")
    patch = lax.rem(t // halves + lax.axis_index("freq"), patches)
    table = jnp.asarray(dft_blocks(length, n_trace))
    waves = digits_low(lax.dynamic_index_in_dim(wavenumbers, patch, 1, keepdims=False))
    places = digits_high(lax.dynamic_index_in_dim(coords, patch, 1, keepdims=False))
    chosen = lax.dynamic_slice(selected, (0, patch, lax.rem(t, halves) * fb), (ITERS, 1, fb)).reshape(-1)
    onehot = (jnp.arange(n_waves, dtype=jnp.int32)[:, None] == chosen[None, :]).astype(jnp.bfloat16)
    picked = jnp.dot(waves, onehot, preferred_element_type=jnp.float32).astype(jnp.bfloat16)
    kd = picked.reshape(16, ITERS, fb).transpose(1, 0, 2)
    my_fold = lax.dynamic_index_in_dim(fold, patch, 0, keepdims=False)
    my_fold = jnp.broadcast_to(my_fold.astype(jnp.float32), (1, fb))
    vmem = pl.BlockSpec(memory_space=pltpu.VMEM)
    hbm = pl.BlockSpec(memory_space=pl.ANY)
    dma = pltpu.SemaphoreType.DMA
    n_buf = min(PRE, n_trace)
    bf16, f32 = jnp.bfloat16, jnp.float32
    recv, coef = pl.pallas_call(
        functools.partial(kernel, n_freq, n_trace),
        out_shape=(jax.ShapeDtypeStruct((n_trace, share, 2 * fb), bf16),
                   jax.ShapeDtypeStruct((n_trace, 8, fb), f32)),
        in_specs=[vmem, hbm, vmem, vmem, vmem, vmem, vmem],
        out_specs=(hbm, vmem),
        scratch_shapes=[
            pltpu.VMEM((2, length, 2 * fb), bf16),
            pltpu.VMEM((n_trace, slots, 2 * fb), bf16),
            pltpu.VMEM((n_trace, slots, 2 * fb), bf16),
            pltpu.VMEM((2 * ITERS, total, fb), f32),
            pltpu.VMEM((2 * total, 2 * fb), bf16),
            pltpu.VMEM((n_buf, share, 2 * total), bf16),
            pltpu.VMEM((n_trace, share, 2 * fb), bf16),
            pltpu.VMEM((8, fb), f32),
            dma((2,)), dma((n_trace,)), dma((n_trace,)), dma,
            dma((n_trace,)), dma((n_trace,)), dma((n_trace,)), dma((n_trace,)), dma,
        ],
        compiler_params=pltpu.CompilerParams(
            collective_id=0, has_side_effects=True, vmem_limit_bytes=58 * 1024 * 1024),
    )(traces[0], table, waves.T, places, places.T, kd, my_fold)
    width = halves * fb
    row = min(width, 128)
    step = min(share, 128)
    rows = patches * 2 * (width // row)
    spectrum = pl.pallas_call(
        functools.partial(unpack, patches),
        out_shape=jax.ShapeDtypeStruct((share * rows, row), f32),
        grid=(share // step,),
        in_specs=[pl.BlockSpec((n_trace, step, 2 * fb), lambda i: (0, i, 0))],
        out_specs=pl.BlockSpec((step * rows, row), lambda i: (i, 0)),
    )(recv)
    spectrum = spectrum.reshape(share, patches, width // row, 2, row).transpose(0, 1, 3, 2, 4)
    spectrum = spectrum.reshape(share, patches, 2, width)
    coef = jnp.roll(coef[:, : 2 * ITERS], halves * lax.axis_index("freq"), axis=0)
    coef = coef.reshape(patches, halves, ITERS, 2, fb).transpose(2, 0, 3, 1, 4)
    return spectrum, coef.reshape(ITERS, patches, 2, width)


def solution(mesh):
    in_specs = (P("freq", "trace", None), P(), P(), P(), P(None, None, "freq"))
    out_specs = (P("trace", None, None, "freq"), P(None, None, None, "freq"))
    return jax.shard_map(local, mesh=mesh, in_specs=in_specs, out_specs=out_specs, check_vma=False)
```
